32 devices in a mesh: col: 4 (over y, x), row: 8 (over z, core).
Axes of the slice: x: 2, y: 2, z: 4, core: 2. Of those that a mesh axis runs over, the one named last changes fastest.
Arguments:
- sigma_ret: float32 [16384, 16384], P('col', 'row'), may hold values from -0.0625 to 0.0625
- sigma_less: float32 [16384, 16384], P('col', 'row'), may hold values from -0.046875 to 0.046875
- green_less: float32 [16384, 1024], P('row', 'col'), may hold values from -6 to 6
- green_ret: float32 [1024, 16384], P(('col', 'row')), may hold values from -6 to 6
Outputs:
- collision: float32 [16384, 1024], P(('col', 'row'))
The draws below stay inside these ranges and needn't reach their ends.
All inputs are finite; a program needn't handle non-finite values.
Results may differ from the reference program's by a relative error of at most 0.00007.
Values sent between devices are 32-bit elements; how exact they have to be, the bound alone decides.
No kernel may reach another device: no remote copies, remote signals or barrier semaphores. Data moves between devices by JAX's collectives and lax.ppermute only.
A program may use at most 192 MiB of HBM per device.

```python
import jax
import jax.numpy as jnp
from jax import lax

M = 16384
W = 1024


def raised(values, key, source, target, blocks, factor):
    owner, partner = [(jnp.arange(values.shape[position]) // (values.shape[position] // blocks)).reshape([-1 if axis == position else 1 for axis in range(values.ndim)]) for position in (source, target)]
    chosen = jax.random.permutation(key, blocks)[partner]
    strong = (owner == chosen) | (owner == (partner + blocks // 2) % blocks)
    return jnp.where(strong, factor * values, values)


def steps_of(rng, extent, pieces, smallest, high):
    factor_of, own = 1.0, jax.random.fold_in(rng, 6)
    for dim, shards_of in pieces:
        heights = jnp.exp(jax.random.uniform(jax.random.fold_in(own, dim), (shards_of,), jnp.float32, smallest / len(pieces), high / len(pieces)))
        factor_of = factor_of * jnp.repeat(heights, extent[dim] // shards_of).reshape([-1 if axis == dim else 1 for axis in range(len(extent))])
    return factor_of


def noise(rng, shape, spread, bound, pieces=(), held_as=jnp.bfloat16):
    drawn = jax.random.normal(rng, shape, jnp.float32) * spread
    if len(pieces) > 0:
        drawn = steps_of(rng, shape, pieces, -0.22, 0.18) * drawn
    return jnp.clip(drawn, min=-bound, max=bound).astype(held_as)


def noise_with(own_key, shape, width, bound, pieces, heavy, kind=jnp.bfloat16):
    result = width * jax.random.normal(own_key, shape, jnp.float32)
    if pieces:
        result = result * steps_of(own_key, shape, pieces, -0.22, 0.18)
    return jnp.clip(raised(result, jax.random.fold_in(own_key, 3), *heavy), -bound, bound).astype(kind)


def setup_inputs(seed: int = 0) -> dict:
    key_of = jax.random.split(jax.random.key(seed), 5)
    sigma_ret = noise_with(key_of[0], (M, M), M ** -0.5, 0.0625, ((0, 4), (1, 8)), (1, 0, 8, 2.0), jnp.float32)
    sigma_less = noise(key_of[1], (M, M), M ** -0.5, 0.046875, ((0, 4), (1, 8)), jnp.float32)
    green_less = noise(key_of[2], (M, W), 1.0, 6.0, ((0, 8), (1, 4)), jnp.float32)
    green_ret = noise(key_of[3], (W, M), 1.0, 6.0, ((0, 32),), jnp.float32)
    return dict(sigma_ret=sigma_ret, sigma_less=sigma_less, green_less=green_less, green_ret=green_ret)


def reference(sigma_ret, sigma_less, green_less, green_ret):
    highest = lax.Precision.HIGHEST
    green_adv = jnp.transpose(green_ret)
    first_term = jnp.dot(sigma_ret, green_less, precision=highest, preferred_element_type=jnp.float32)
    second_term = jnp.dot(sigma_less, green_adv, precision=highest, preferred_element_type=jnp.float32)
    return first_term + second_term
```

```python
import functools

import jax
import jax.numpy as jnp
from jax import lax
from jax.experimental import pallas as pl
from jax.experimental.pallas import tpu as pltpu
from jax.sharding import PartitionSpec as P

F32 = jnp.float32
BF16 = jnp.bfloat16


def bits_of(extent):
    assert extent & (extent - 1) == 0
    return [1 << place for place in range(extent.bit_length() - 1)]


def halving_order(extent):
    order = [0]
    for bit in reversed(bits_of(extent)):
        order = [distance | bit for distance in order] + order
    return order


def cuts(extent, parts, unit):
    edges = [extent * part // parts // unit * unit for part in range(parts)] + [extent]
    return list(zip(edges[:-1], edges[1:]))


def split(values):
    high = values.astype(BF16)
    return high, (values - high.astype(F32)).astype(BF16)


def term_kernel(mirrored, n_parts, n_added, pieces, tiles, where, sigma, *refs):
    parts, added = refs[:n_parts], refs[n_parts : n_parts + n_added]
    out, high, low = refs[n_parts + n_added : n_parts + n_added + 3]

    @pl.when(pl.program_id(0) == 0)
    def _():
        start = 0
        if mirrored:
            whole = refs[-1]
            for part in parts:
                for begin in range(0, part.shape[0], pieces):
                    distance = (start + begin) // pieces
                    place = pl.multiple_of((where[0] ^ distance) * pieces, pieces)
                    whole[pl.ds(place, pieces), :] = part[begin : begin + pieces, :]
                start += part.shape[0]
            high[...], low[...] = split(whole[...])
        else:
            for part in parts:
                rows = slice(start, start + part.shape[0])
                high[rows, :], low[rows, :] = split(part[...])
                start += part.shape[0]

    dims = (((1,), (1 if mirrored else 0,)), ((), ()))
    product = functools.partial(lax.dot_general, dimension_numbers=dims, preferred_element_type=F32)
    sigma_high, sigma_low = split(sigma[...])
    total = product(sigma_high, high[...])
    total += product(sigma_high, low[...])
    total += product(sigma_low, high[...])
    for other in added:
        total += other[...]
    out[...] = total


def term(sigma, parts, tiles, where, added, mirrored, pieces, tile, name):
    depth = sigma.shape[1]
    columns = sum(part.shape[0] for part in parts) if mirrored else parts[0].shape[1]
    held = (columns, depth) if mirrored else (depth, columns)
    steps = tiles.shape[0]
    whole = lambda shape: pl.BlockSpec(shape, lambda i, t, w: (0, 0), pipeline_mode=pl.Buffered(1))
    scratch = [pltpu.VMEM(held, BF16), pltpu.VMEM(held, BF16)]
    if mirrored:
        scratch.append(pltpu.VMEM(held, F32))
    return pl.pallas_call(
        functools.partial(term_kernel, mirrored, len(parts), len(added), pieces),
        out_shape=jax.ShapeDtypeStruct((steps * tile, columns), F32),
        grid_spec=pltpu.PrefetchScalarGridSpec(
            num_scalar_prefetch=2,
            grid=(steps,),
            in_specs=[pl.BlockSpec((tile, depth), lambda i, t, w: (t[i], 0))]
            + [whole(part.shape) for part in parts]
            + [pl.BlockSpec((tile, columns), lambda i, t, w, o=offset // tile: (i + o, 0)) for _, offset in added],
            out_specs=pl.BlockSpec((tile, columns), lambda i, t, w: (i, 0)),
            scratch_shapes=scratch,
        ),
        compiler_params=pltpu.CompilerParams(vmem_limit_bytes=40 << 20),
        cost_estimate=pl.CostEstimate(
            flops=6 * steps * tile * depth * columns,
            bytes_accessed=4 * steps * tile * (depth + columns * (1 + len(added))) + 4 * depth * columns,
            transcendentals=0,
        ),
        name=name,
    )(tiles, where, sigma, *parts, *[array for array, _ in added])


def gather_panels(own, extent, unit):
    held = {0: [own]}
    for distance in sorted(range(1, extent), key=lambda d: (bin(d).count("1"), d)):
        bits = [bit for bit in bits_of(extent) if distance & bit]
        parts = []
        for bit, (begin, end) in zip(bits, cuts(own.shape[0], len(bits), unit)):
            source = held[distance ^ bit]
            source = source[0] if len(source) == 1 else jnp.concatenate(source, axis=0)
            pairs = [(i, i ^ bit) for i in range(extent)]
            parts.append(lax.ppermute(source[begin:end], "col", pairs))
        held[distance] = parts
    return held


def on_device(sigma_ret, sigma_less, green_less, green_ret):
    n_col, n_row = lax.axis_size("col"), lax.axis_size("row")
    col, row = lax.axis_index("col"), lax.axis_index("row")
    rows, depth = sigma_ret.shape
    columns = green_less.shape[1]
    block, pieces = rows // n_row, green_ret.shape[0]
    tile = min(block, 512)

    received = []
    for distance in range(n_row):
        piece = lax.dynamic_slice(green_ret, (0, (row ^ distance) * depth), (pieces, depth))
        if distance:
            piece = lax.ppermute(piece, "row", [(i, i ^ distance) for i in range(n_row)])
        received.append(piece)
    mirrored_own = jnp.concatenate(received, axis=0)

    lesser = gather_panels(green_less, n_col, 16)
    mirrored = gather_panels(mirrored_own, n_col, pieces)

    per_block = block // tile
    order = jnp.asarray(halving_order(n_row), jnp.int32)
    tiles = (((order ^ row) * per_block)[:, None] + jnp.arange(per_block, dtype=jnp.int32)).reshape(-1)
    where = row.astype(jnp.int32).reshape(1)
    half = tiles.shape[0] // 2

    out = jnp.zeros((block, n_col * columns), F32)
    for distance in sorted(range(n_col), key=lambda d: (bin(d).count("1"), d)):
        first = term(sigma_ret, lesser[distance], tiles, where, [], False, pieces, tile, "first_term")
        second = functools.partial(term, sigma_less, mirrored[distance], mirrored=True, pieces=pieces, tile=tile)
        sent = second(tiles[:half], where, [(first, 0)], name="second_sent")
        came = lax.ppermute(sent, "row", [(i, i ^ 1) for i in range(n_row)])
        kept = second(tiles[half:], where, [(first, rows // 2)], name="second_kept")
        sums = [kept, came]
        for bit in bits_of(n_row)[1:]:
            middle = sums[0].shape[0] // 2
            sent = functools.reduce(jnp.add, [array[:middle] for array in sums])
            sums = [array[middle:] for array in sums]
            sums.append(lax.ppermute(sent, "row", [(i, i ^ bit) for i in range(n_row)]))
        final = functools.reduce(jnp.add, sums)
        out = lax.dynamic_update_slice(out, final, (0, (col ^ distance) * columns))
    return out


def solution(mesh):
    placed = (P("col", "row"), P("col", "row"), P("row", "col"), P(("col", "row"), None))
    return jax.shard_map(
        on_device, mesh=mesh, in_specs=placed, out_specs=P(("col", "row"), None), check_vma=False
    )
```

```python
import functools

import jax
import jax.numpy as jnp
from jax import lax
from jax.experimental import pallas as pl
from jax.experimental.pallas import tpu as pltpu
from jax.sharding import PartitionSpec as P

F32 = jnp.float32
BF16 = jnp.bfloat16


def bits_of(extent):
    assert extent & (extent - 1) == 0
    return [1 << place for place in range(extent.bit_length() - 1)]


def halving_order(extent):
    order = [0]
    for bit in reversed(bits_of(extent)):
        order = [distance | bit for distance in order] + order
    return order


def split(values):
    high = values.astype(BF16)
    return high, (values - high.astype(F32)).astype(BF16)


def term_kernel(kinds, streams, n_parts, n_added, n_after, tiles, *refs):
    held, refs = [], list(refs)

    def take(count):
        taken = refs[:count]
        del refs[:count]
        return taken

    for _ in kinds:
        held.append((take(streams), take(n_parts)))
    added, _, out = take(n_added), take(n_after), take(1)[0]
    panels = [take(2) for _ in kinds]

    @pl.when(pl.program_id(0) == 0)
    def _():
        for mirrored, (_, parts), (high_panel, low_panel) in zip(kinds, held, panels):
            column = 0
            for part in parts:
                columns = slice(column, column + part.shape[0 if mirrored else 1])
                place = (columns, slice(None)) if mirrored else (slice(None), columns)
                high_panel[place], low_panel[place] = split(part[...])
                column = columns.stop

    total = None
    for mirrored, (sigma, _), (high_panel, low_panel) in zip(kinds, held, panels):
        dims = (((1,), (1 if mirrored else 0,)), ((), ()))
        halves = [split(stream[...]) for stream in sigma]
        high, low = [jnp.concatenate([half[which] for half in halves], axis=0) for which in range(2)]
        for left, right in ((high, high_panel), (high, low_panel), (low, high_panel)):
            product = lax.dot_general(left, right[...], dims, preferred_element_type=F32)
            total = product if total is None else total + product
    for other in added:
        total += other[...]
    out[...] = total


def sum_of_terms(terms, columns, tiles, added, after, tile, name):
    depth = terms[0][0].shape[1]
    n_parts = len(terms[0][1])
    near = columns // n_parts
    steps, streams = tiles.shape[0], 1
    in_specs, operands, scratch = [], [], []
    for sigma, parts, mirrored in terms:
        for j in range(streams):
            in_specs.append(pl.BlockSpec((tile // streams, depth), lambda i, t, j=j: (t[i] * streams + j, 0)))
            operands.append(sigma)
        for part, place in parts:
            shape, index = ((near, depth), (place, 0)) if mirrored else ((depth, near), (0, place))
            in_specs.append(pl.BlockSpec(shape, lambda i, t, index=index: index, pipeline_mode=pl.Buffered(1)))
            operands.append(part)
        scratch += [pltpu.VMEM((columns, depth) if mirrored else (depth, columns), BF16)] * 2
    for array, offset in added:
        in_specs.append(pl.BlockSpec((tile, columns), lambda i, t, o=offset // tile: (i + o, 0)))
        operands.append(array)
    in_specs += [pl.BlockSpec(memory_space=pl.ANY) for _ in after]
    kinds = [mirrored for _, _, mirrored in terms]
    return pl.pallas_call(
        functools.partial(term_kernel, kinds, streams, n_parts, len(added), len(after)),
        out_shape=jax.ShapeDtypeStruct((steps * tile, columns), F32),
        grid_spec=pltpu.PrefetchScalarGridSpec(
            num_scalar_prefetch=1,
            grid=(steps,),
            in_specs=in_specs,
            out_specs=pl.BlockSpec((tile, columns), lambda i, t: (i, 0)),
            scratch_shapes=scratch,
        ),
        compiler_params=pltpu.CompilerParams(vmem_limit_bytes=40 << 20),
        cost_estimate=pl.CostEstimate(
            flops=48 * len(terms) * steps * tile * depth * columns,
            bytes_accessed=4 * len(terms) * steps * tile * depth,
            transcendentals=0,
        ),
        name=name,
    )(tiles, *operands, *after)


def place_copies(sources, shapes, moves, name, after=()):
    def kernel(*refs):
        for when, source, target in moves(refs[: len(sources)], refs[len(sources) + len(after) :]):

            @pl.when(when)
            def _(source=source, target=target):
                target[...] = source[...]

    return pl.pallas_call(
        kernel,
        out_shape=[jax.ShapeDtypeStruct(shape, F32) for shape in shapes],
        in_specs=[pl.BlockSpec(memory_space=pltpu.VMEM) for _ in sources]
        + [pl.BlockSpec(memory_space=pl.ANY) for _ in after],
        out_specs=[pl.BlockSpec(memory_space=pltpu.VMEM) for _ in shapes],
        compiler_params=pltpu.CompilerParams(vmem_limit_bytes=60 << 20),
        name=name,
    )(*sources, *after)


def hold(values, after):
    return pl.pallas_call(
        lambda *refs: None,
        out_shape=jax.ShapeDtypeStruct(values.shape, values.dtype),
        in_specs=[pl.BlockSpec(memory_space=pl.ANY)] * (1 + len(after)),
        out_specs=pl.BlockSpec(memory_space=pl.ANY),
        input_output_aliases={0: 0},
        name="hold",
    )(values, *after)


def on_device(sigma_ret, sigma_less, green_less, green_ret):
    n_col, n_row = lax.axis_size("col"), lax.axis_size("row")
    col, row = lax.axis_index("col"), lax.axis_index("row")
    rows, depth = sigma_ret.shape
    columns = green_less.shape[1]
    block, pieces = rows // n_row, green_ret.shape[0]
    tile = min(block, 512)
    near = columns // 2
    chips = n_row // 2

    to_row = lambda values, distance: lax.ppermute(values, "row", [(i, i ^ distance) for i in range(n_row)])
    to_col = lambda values, distance: lax.ppermute(values, "col", [(i, i ^ distance) for i in range(n_col)])

    col_bits = bits_of(n_col)
    blocks = [[(0, 0), (0, 1)]] + [[(bit, part) for bit in col_bits] for part in range(2) if col_bits]
    far = sorted([d for d in range(n_col) if d & (d - 1)], key=lambda d: (bin(d).count("1"), d))
    blocks += [[(d, 0), (d, 1)] for d in far]

    def bring(panels, members):
        for distance, part in members:
            bit = distance & -distance if part == 0 else 1 << (distance.bit_length() - 1)
            panels[distance, part] = to_col(panels[distance ^ bit, part], bit)

    def piece(ref, owner):
        return ref.at[:, pl.ds(pl.multiple_of(owner * depth, depth), depth)]

    def rows_of(ref, place, extent):
        return ref.at[pl.ds(pl.multiple_of(place * extent, extent), extent)]

    def crossing_moves(sources, results):
        core = lax.axis_index("row") % 2
        return [
            (True, piece(sources[0], 2 * other + 1 - core), rows_of(results[0], other, pieces)) for other in range(chips)
        ]

    def pair_moves(sources, results):
        chip, core = lax.axis_index("row") // 2, lax.axis_index("row") % 2
        moves = []
        for distance in range(chips):
            other = chip ^ distance
            moves.append((True, piece(sources[0], 2 * other + core), rows_of(results[distance], core, pieces)))
            moves.append((True, rows_of(sources[1], other, pieces), rows_of(results[distance], 1 - core, pieces)))
        return moves

    def panel_moves(sources, results):
        chip, moves = lax.axis_index("row") // 2, []
        for distance in range(chips):
            other = chip ^ distance
            for half in range(2):
                target = rows_of(results[half], other % (chips // 2), 2 * pieces)
                moves.append((other // (chips // 2) == half, sources[distance], target))
        return moves

    crossing = place_copies([green_ret], [(chips * pieces, depth)], crossing_moves, "crossing")[0]
    crossing = to_row(crossing, 1)
    pairs = place_copies([green_ret, crossing], [(2 * pieces, depth)] * chips, pair_moves, "pairs")
    halves = {(0, part): green_less[:, part * near : (part + 1) * near] for part in range(2)}
    if col_bits:
        bring(halves, blocks[1])
    lesser = {(0, part): (green_less, part) if near % 128 == 0 else (halves[0, part], 0) for part in range(2)}

    order = jnp.asarray(halving_order(n_row), jnp.int32)

    def tiles_of(tile, share, shares):
        count = block // tile // shares
        within = share * count + jnp.arange(count, dtype=jnp.int32)
        return (((order ^ row) * (block // tile))[:, None] + within).reshape(-1)

    after = list(pairs[1:])

    def run(terms, members, tiles, added, tile, name):
        result = sum_of_terms(terms, near * len(members), tiles, added, after, tile, name)
        after[:] = [result]
        return result

    def first_of(members):
        return sigma_ret, [lesser.get(m) or (halves[m], 0) for m in members], False

    def second_of(members):
        return sigma_less, [(mirrored[m], 0) for m in members], True

    def run_first(place):
        return run([first_of(blocks[place])], blocks[place], tiles_of(tile, 0, 1), [], tile, "first_term")

    def run_half(place, kept, share, shares):
        members, height = blocks[place], tile // (2 if place > 1 else 1)
        tiles = tiles_of(height, share, shares)
        half = tiles.shape[0] // 2
        tiles = tiles[half:] if kept else tiles[:half]
        if place in firsts:
            added = [(firsts[place], rows // 2 if kept else 0)]
            return run([second_of(members)], members, tiles, added, height, "second_term")
        return run([first_of(members), second_of(members)], members, tiles, [], height, "both_terms")

    def halve(sums, bits):
        if not bits:
            return sums, bits
        middle = sums[0].shape[0] // 2
        sent = functools.reduce(jnp.add, [array[:middle] for array in sums])
        after.append(sent)
        return [array[middle:] for array in sums] + [to_row(sent, bits[0])], bits[1:]

    row_bits = bits_of(n_row)
    firsts, going = {0: run_first(0)}, []
    if col_bits:
        halves[0, 1] = hold(halves[0, 1], after)
        bring(halves, blocks[2])
        firsts[1] = run_first(1)

    came = [pairs[0]] + [to_row(pairs[distance], 2 * distance) for distance in range(1, chips)]
    shapes = [(columns // 2, depth)] * 2
    panels = place_copies(came, shapes, panel_moves, "mirrored", after)
    mirrored = {(0, part): panels[part] for part in range(2)}
    bring(mirrored, blocks[1] if col_bits else [])

    def relay(panels, part, after):
        for distance in far:
            bit = distance & -distance if part == 0 else 1 << (distance.bit_length() - 1)
            source = distance ^ bit, part
            if source in blocks[1] + blocks[2]:
                panels[source] = hold(panels[source], after)
            bring(panels, [(distance, part)])

    def advance(going, out):
        last = [which for which, each in enumerate(going) if each is not None and not each[2]]
        for which, each in enumerate(going):
            if each is not None and each[2]:
                going[which] = [each[0], *halve([hold(each[1][0], after), *each[1][1:]], each[2])]
        for which in last:
            (place, start), sums, _ = going[which]
            going[which] = None
            final = functools.reduce(jnp.add, [hold(sums[0], after), *sums[1:]])
            for index, (distance, part) in enumerate(blocks[place]):
                values = final[:, index * near : (index + 1) * near]
                out = lax.dynamic_update_slice(out, values, (start, (col ^ distance) * columns + part * near))
            after.append(out)
        return out

    out = jnp.zeros((block, n_col * columns), F32)
    for place, members in enumerate(blocks):
        if place == 1:
            after.extend(halves[member] for member in blocks[2])
            mirrored[0, 1] = hold(mirrored[0, 1], after)
            bring(mirrored, blocks[2])
            relay(halves, 0, after)
        if place == 2:
            relay(mirrored, 0, after)
            relay(mirrored, 1, after)
            relay(halves, 1, after)
        shares = 2 if place == len(blocks) - 1 and place > 1 else 1
        for share in range(shares):
            sent = run_half(place, False, share, shares)
            came = to_row(sent, 1)
            if place == 2:
                after.extend(halves[distance, 0] for distance in far)
            kept = run_half(place, True, share, shares)
            now = halve([kept, came], row_bits[1:])
            if place != 1:
                out = advance(going, out)
            going.append([(place, share * (block // shares)), *now])
    while any(each is not None for each in going):
        out = advance(going, out)
    return out


def solution(mesh):
    placed = (P("col", "row"), P("col", "row"), P("row", "col"), P(("col", "row"), None))
    return jax.shard_map(
        on_device, mesh=mesh, in_specs=placed, out_specs=P(("col", "row"), None), check_vma=False
    )
```

```python
import functools

import jax
import jax.numpy as jnp
from jax import lax
from jax.experimental import pallas as pl
from jax.experimental.pallas import tpu as pltpu
from jax.sharding import PartitionSpec as P

F32 = jnp.float32
BF16 = jnp.bfloat16


def bits_of(extent):
    assert extent & (extent - 1) == 0
    return [1 << place for place in range(extent.bit_length() - 1)]


def halving_order(extent):
    order = [0]
    for bit in reversed(bits_of(extent)):
        order = [distance | bit for distance in order] + order
    return order


def split(values):
    high = values.astype(BF16)
    return high, (values - high.astype(F32)).astype(BF16)


def term_kernel(kinds, streams, n_parts, n_added, n_after, tiles, *refs):
    held, refs = [], list(refs)

    def take(count):
        taken = refs[:count]
        del refs[:count]
        return taken

    for _ in kinds:
        held.append((take(streams), take(n_parts)))
    added, _, out = take(n_added), take(n_after), take(1)[0]
    panels = [take(2) for _ in kinds]

    @pl.when(pl.program_id(0) == 0)
    def _():
        for mirrored, (_, parts), (high_panel, low_panel) in zip(kinds, held, panels):
            column = 0
            for part in parts:
                columns = slice(column, column + part.shape[0 if mirrored else 1])
                place = (columns, slice(None)) if mirrored else (slice(None), columns)
                high_panel[place], low_panel[place] = split(part[...])
                column = columns.stop

    total = None
    for mirrored, (sigma, _), (high_panel, low_panel) in zip(kinds, held, panels):
        dims = (((1,), (1 if mirrored else 0,)), ((), ()))
        halves = [split(stream[...]) for stream in sigma]
        high, low = [jnp.concatenate([half[which] for half in halves], axis=0) for which in range(2)]
        for left, right in ((high, high_panel), (high, low_panel), (low, high_panel)):
            product = lax.dot_general(left, right[...], dims, preferred_element_type=F32)
            total = product if total is None else total + product
    for other in added:
        total += other[...]
    out[...] = total


def sum_of_terms(terms, columns, tiles, added, after, tile, name):
    depth = terms[0][0].shape[1]
    n_parts = len(terms[0][1])
    near = columns // n_parts
    steps, streams = tiles.shape[0], 1
    in_specs, operands, scratch = [], [], []
    for sigma, parts, mirrored in terms:
        for j in range(streams):
            in_specs.append(pl.BlockSpec((tile // streams, depth), lambda i, t, j=j: (t[i] * streams + j, 0)))
            operands.append(sigma)
        for part, place in parts:
            shape, index = ((near, depth), (place, 0)) if mirrored else ((depth, near), (0, place))
            in_specs.append(pl.BlockSpec(shape, lambda i, t, index=index: index, pipeline_mode=pl.Buffered(1)))
            operands.append(part)
        scratch += [pltpu.VMEM((columns, depth) if mirrored else (depth, columns), BF16)] * 2
    for array, offset in added:
        in_specs.append(pl.BlockSpec((tile, columns), lambda i, t, o=offset // tile: (i + o, 0)))
        operands.append(array)
    in_specs += [pl.BlockSpec(memory_space=pl.ANY) for _ in after]
    kinds = [mirrored for _, _, mirrored in terms]
    return pl.pallas_call(
        functools.partial(term_kernel, kinds, streams, n_parts, len(added), len(after)),
        out_shape=jax.ShapeDtypeStruct((steps * tile, columns), F32),
        grid_spec=pltpu.PrefetchScalarGridSpec(
            num_scalar_prefetch=1,
            grid=(steps,),
            in_specs=in_specs,
            out_specs=pl.BlockSpec((tile, columns), lambda i, t: (i, 0)),
            scratch_shapes=scratch,
        ),
        compiler_params=pltpu.CompilerParams(vmem_limit_bytes=60 << 20),
        cost_estimate=pl.CostEstimate(
            flops=48 * len(terms) * steps * tile * depth * columns,
            bytes_accessed=4 * len(terms) * steps * tile * depth,
            transcendentals=0,
        ),
        name=name,
    )(tiles, *operands, *after)


def place_copies(sources, shapes, moves, name, after=()):
    def kernel(*refs):
        for when, source, target in moves(refs[: len(sources)], refs[len(sources) + len(after) :]):

            @pl.when(when)
            def _(source=source, target=target):
                target[...] = source[...]

    return pl.pallas_call(
        kernel,
        out_shape=[jax.ShapeDtypeStruct(shape, F32) for shape in shapes],
        in_specs=[pl.BlockSpec(memory_space=pltpu.VMEM) for _ in sources]
        + [pl.BlockSpec(memory_space=pl.ANY) for _ in after],
        out_specs=[pl.BlockSpec(memory_space=pltpu.VMEM) for _ in shapes],
        compiler_params=pltpu.CompilerParams(vmem_limit_bytes=60 << 20),
        name=name,
    )(*sources, *after)


def hold(values, after):
    return pl.pallas_call(
        lambda *refs: None,
        out_shape=jax.ShapeDtypeStruct(values.shape, values.dtype),
        in_specs=[pl.BlockSpec(memory_space=pl.ANY)] * (1 + len(after)),
        out_specs=pl.BlockSpec(memory_space=pl.ANY),
        input_output_aliases={0: 0},
        name="hold",
    )(values, *after)


def on_device(sigma_ret, sigma_less, green_less, green_ret):
    n_col, n_row = lax.axis_size("col"), lax.axis_size("row")
    col, row = lax.axis_index("col"), lax.axis_index("row")
    rows, depth = sigma_ret.shape
    columns = green_less.shape[1]
    block, pieces = rows // n_row, green_ret.shape[0]
    tile = min(block, 512)
    near = columns // 2
    chips = n_row // 2

    to_row = lambda values, distance: lax.ppermute(values, "row", [(i, i ^ distance) for i in range(n_row)])
    to_col = lambda values, distance: lax.ppermute(values, "col", [(i, i ^ distance) for i in range(n_col)])

    col_bits = bits_of(n_col)
    blocks = [[(0, 0), (0, 1)]] + [[(bit, part) for bit in col_bits] for part in range(2) if col_bits]
    far = sorted([d for d in range(n_col) if d & (d - 1)], key=lambda d: (bin(d).count("1"), d))
    blocks += [[(d, 0), (d, 1)] for d in far]

    def bring(panels, members):
        for distance, part in members:
            bit = distance & -distance if part == 0 else 1 << (distance.bit_length() - 1)
            panels[distance, part] = to_col(panels[distance ^ bit, part], bit)

    def piece(ref, owner):
        return ref.at[:, pl.ds(pl.multiple_of(owner * depth, depth), depth)]

    def rows_of(ref, place, extent):
        return ref.at[pl.ds(pl.multiple_of(place * extent, extent), extent)]

    def crossing_moves(sources, results):
        core = lax.axis_index("row") % 2
        return [
            (True, piece(sources[0], 2 * other + 1 - core), rows_of(results[0], other, pieces)) for other in range(chips)
        ]

    def pair_moves(sources, results):
        chip, core = lax.axis_index("row") // 2, lax.axis_index("row") % 2
        moves = []
        for distance in range(chips):
            other = chip ^ distance
            moves.append((True, piece(sources[0], 2 * other + core), rows_of(results[distance], core, pieces)))
            moves.append((True, rows_of(sources[1], other, pieces), rows_of(results[distance], 1 - core, pieces)))
        return moves

    def panel_moves(sources, results):
        chip, moves = lax.axis_index("row") // 2, []
        for distance in range(chips):
            other = chip ^ distance
            for half in range(2):
                target = rows_of(results[half], other % (chips // 2), 2 * pieces)
                moves.append((other // (chips // 2) == half, sources[distance], target))
        return moves

    crossing = place_copies([green_ret], [(chips * pieces, depth)], crossing_moves, "crossing")[0]
    crossing = to_row(crossing, 1)
    pairs = place_copies([green_ret, crossing], [(2 * pieces, depth)] * chips, pair_moves, "pairs")
    halves = {(0, part): green_less[:, part * near : (part + 1) * near] for part in range(2)}
    if col_bits:
        bring(halves, blocks[1])
    lesser = {(0, part): (green_less, part) if near % 128 == 0 else (halves[0, part], 0) for part in range(2)}

    order = jnp.asarray(halving_order(n_row), jnp.int32)

    def tiles_of(tile, share, shares):
        count = block // tile // shares
        within = share * count + jnp.arange(count, dtype=jnp.int32)
        return (((order ^ row) * (block // tile))[:, None] + within).reshape(-1)

    after = list(pairs[1:])

    def run(terms, members, tiles, added, tile, name):
        result = sum_of_terms(terms, near * len(members), tiles, added, after, tile, name)
        after[:] = [result]
        return result

    def first_of(members):
        return sigma_ret, [lesser.get(m) or (halves[m], 0) for m in members], False

    def second_of(members):
        return sigma_less, [(mirrored[m], 0) for m in members], True

    def run_first(place):
        return run([first_of(blocks[place])], blocks[place], tiles_of(tile, 0, 1), [], tile, "first_term")

    def run_half(place, kept, share, shares):
        members, height = blocks[place], tile // (2 if place > 1 else 1)
        tiles = tiles_of(height, share, shares)
        half = tiles.shape[0] // 2
        tiles = tiles[half:] if kept else tiles[:half]
        if place in firsts:
            added = [(firsts[place], rows // 2 if kept else 0)]
            return run([second_of(members)], members, tiles, added, height, "second_term")
        return run([first_of(members), second_of(members)], members, tiles, [], height, "both_terms")

    def halve(sums, bits):
        if not bits:
            return sums, bits
        middle = sums[0].shape[0] // 2
        sent = functools.reduce(jnp.add, [array[:middle] for array in sums])
        after.append(sent)
        return [array[middle:] for array in sums] + [to_row(sent, bits[0])], bits[1:]

    row_bits = bits_of(n_row)
    firsts, going = {0: run_first(0)}, []
    if col_bits:
        halves[0, 1] = hold(halves[0, 1], after)
        bring(halves, blocks[2])
        firsts[1] = run_first(1)

    came = [pairs[0]] + [to_row(pairs[distance], 2 * distance) for distance in range(1, chips)]
    shapes = [(columns // 2, depth)] * 2
    panels = place_copies(came, shapes, panel_moves, "mirrored", after)
    mirrored = {(0, part): panels[part] for part in range(2)}
    bring(mirrored, blocks[1] if col_bits else [])

    def relay(panels, part, after):
        for distance in far:
            bit = distance & -distance if part == 0 else 1 << (distance.bit_length() - 1)
            source = distance ^ bit, part
            if source in blocks[1] + blocks[2]:
                panels[source] = hold(panels[source], after)
            bring(panels, [(distance, part)])

    def advance(going, out):
        last = [which for which, each in enumerate(going) if each is not None and not each[2]]
        for which, each in enumerate(going):
            if each is not None and each[2]:
                going[which] = [each[0], *halve([hold(each[1][0], after), *each[1][1:]], each[2])]
        for which in last:
            (place, start), sums, _ = going[which]
            going[which] = None
            final = functools.reduce(jnp.add, [hold(sums[0], after), *sums[1:]])
            for index, (distance, part) in enumerate(blocks[place]):
                values = final[:, index * near : (index + 1) * near]
                out = lax.dynamic_update_slice(out, values, (start, (col ^ distance) * columns + part * near))
            after.append(out)
        return out

    def halve_sums(going):
        where, sums, bits = going[0]
        sums = [hold(sums[0], after), *sums[1:]]
        middle = sums[0].shape[0] // 2
        sent = functools.reduce(jnp.add, [array[:middle] for array in sums])
        after.append(sent)
        return sent, [array[middle:] for array in sums]

    def send_later(going, later):
        where, _, bits = going[0]
        sent, kept = later
        going[0] = [where, [*kept, to_row(hold(sent, after), bits[0])], bits[1:]]

    out = jnp.zeros((block, n_col * columns), F32)
    for place, members in enumerate(blocks):
        if place == 1:
            after.extend(halves[member] for member in blocks[2])
            mirrored[0, 1] = hold(mirrored[0, 1], after)
            bring(mirrored, blocks[2])
            relay(halves, 0, after)
        if place == 2:
            relay(mirrored, 0, after)
            relay(mirrored, 1, after)
            relay(halves, 1, after)
        shares = 2 if place == len(blocks) - 1 and place > 1 else 1
        for share in range(shares):
            sent = run_half(place, False, share, shares)
            came = to_row(sent, 1)
            if place == 2:
                after.extend(halves[distance, 0] for distance in far)
            kept = run_half(place, True, share, shares)
            now = halve([kept, came], row_bits[1:])
            if place == 1:
                later = halve_sums(going)
            else:
                if place == 2:
                    send_later(going, later)
                    going[1:] = [[each[0], *halve([hold(each[1][0], after), *each[1][1:]], each[2])] for each in going[1:]]
                else:
                    out = advance(going, out)
            going.append([(place, share * (block // shares)), *now])
    while any(each is not None for each in going):
        out = advance(going, out)
    return out


def solution(mesh):
    placed = (P("col", "row"), P("col", "row"), P("row", "col"), P(("col", "row"), None))
    return jax.shard_map(
        on_device, mesh=mesh, in_specs=placed, out_specs=P(("col", "row"), None), check_vma=False
    )
```

```python
import functools

import jax
import jax.numpy as jnp
from jax import lax
from jax.experimental import pallas as pl
from jax.experimental.pallas import tpu as pltpu
from jax.sharding import PartitionSpec as P

F32 = jnp.float32
BF16 = jnp.bfloat16


def bits_of(extent):
    assert extent & (extent - 1) == 0
    return [1 << place for place in range(extent.bit_length() - 1)]


def halving_order(extent):
    order = [0]
    for bit in reversed(bits_of(extent)):
        order = [distance | bit for distance in order] + order
    return order


def split(values):
    high = values.astype(BF16)
    return high, (values - high.astype(F32)).astype(BF16)


def term_kernel(kinds, streams, n_parts, n_added, n_after, tiles, *refs):
    held, refs = [], list(refs)

    def take(count):
        taken = refs[:count]
        del refs[:count]
        return taken

    for _ in kinds:
        held.append((take(streams), take(n_parts)))
    added, _, out = take(n_added), take(n_after), take(1)[0]
    panels = [take(2) for _ in kinds]

    @pl.when(pl.program_id(0) == 0)
    def _():
        for mirrored, (_, parts), (high_panel, low_panel) in zip(kinds, held, panels):
            column = 0
            for part in parts:
                columns = slice(column, column + part.shape[0 if mirrored else 1])
                place = (columns, slice(None)) if mirrored else (slice(None), columns)
                high_panel[place], low_panel[place] = split(part[...])
                column = columns.stop

    total = None
    for mirrored, (sigma, _), (high_panel, low_panel) in zip(kinds, held, panels):
        dims = (((1,), (1 if mirrored else 0,)), ((), ()))
        halves = [split(stream[...]) for stream in sigma]
        high, low = [jnp.concatenate([half[which] for half in halves], axis=0) for which in range(2)]
        for left, right in ((high, high_panel), (high, low_panel), (low, high_panel)):
            product = lax.dot_general(left, right[...], dims, preferred_element_type=F32)
            total = product if total is None else total + product
    for other in added:
        total += other[...]
    out[...] = total


def sum_of_terms(terms, columns, tiles, added, after, tile, name):
    depth = terms[0][0].shape[1]
    n_parts = len(terms[0][1])
    near = columns // n_parts
    steps, streams = tiles.shape[0], 1
    in_specs, operands, scratch = [], [], []
    for sigma, parts, mirrored in terms:
        for j in range(streams):
            in_specs.append(pl.BlockSpec((tile // streams, depth), lambda i, t, j=j: (t[i] * streams + j, 0)))
            operands.append(sigma)
        for part, place in parts:
            shape, index = ((near, depth), (place, 0)) if mirrored else ((depth, near), (0, place))
            in_specs.append(pl.BlockSpec(shape, lambda i, t, index=index: index, pipeline_mode=pl.Buffered(1)))
            operands.append(part)
        scratch += [pltpu.VMEM((columns, depth) if mirrored else (depth, columns), BF16)] * 2
    for array, offset in added:
        in_specs.append(pl.BlockSpec((tile, columns), lambda i, t, o=offset // tile: (i + o, 0)))
        operands.append(array)
    in_specs += [pl.BlockSpec(memory_space=pl.ANY) for _ in after]
    kinds = [mirrored for _, _, mirrored in terms]
    return pl.pallas_call(
        functools.partial(term_kernel, kinds, streams, n_parts, len(added), len(after)),
        out_shape=jax.ShapeDtypeStruct((steps * tile, columns), F32),
        grid_spec=pltpu.PrefetchScalarGridSpec(
            num_scalar_prefetch=1,
            grid=(steps,),
            in_specs=in_specs,
            out_specs=pl.BlockSpec((tile, columns), lambda i, t: (i, 0)),
            scratch_shapes=scratch,
        ),
        compiler_params=pltpu.CompilerParams(vmem_limit_bytes=60 << 20),
        cost_estimate=pl.CostEstimate(
            flops=48 * len(terms) * steps * tile * depth * columns,
            bytes_accessed=4 * len(terms) * steps * tile * depth,
            transcendentals=0,
        ),
        name=name,
    )(tiles, *operands, *after)


def place_copies(sources, shapes, moves, name, after=()):
    def kernel(*refs):
        for when, source, target in moves(refs[: len(sources)], refs[len(sources) + len(after) :]):

            @pl.when(when)
            def _(source=source, target=target):
                target[...] = source[...]

    return pl.pallas_call(
        kernel,
        out_shape=[jax.ShapeDtypeStruct(shape, F32) for shape in shapes],
        in_specs=[pl.BlockSpec(memory_space=pltpu.VMEM) for _ in sources]
        + [pl.BlockSpec(memory_space=pl.ANY) for _ in after],
        out_specs=[pl.BlockSpec(memory_space=pltpu.VMEM) for _ in shapes],
        compiler_params=pltpu.CompilerParams(vmem_limit_bytes=60 << 20),
        name=name,
    )(*sources, *after)


def hold(values, after):
    return pl.pallas_call(
        lambda *refs: None,
        out_shape=jax.ShapeDtypeStruct(values.shape, values.dtype),
        in_specs=[pl.BlockSpec(memory_space=pl.ANY)] * (1 + len(after)),
        out_specs=pl.BlockSpec(memory_space=pl.ANY),
        input_output_aliases={0: 0},
        name="hold",
    )(values, *after)


def on_device(sigma_ret, sigma_less, green_less, green_ret):
    n_col, n_row = lax.axis_size("col"), lax.axis_size("row")
    col, row = lax.axis_index("col"), lax.axis_index("row")
    rows, depth = sigma_ret.shape
    columns = green_less.shape[1]
    block, pieces = rows // n_row, green_ret.shape[0]
    tile = min(block, 512)
    near = columns // 2
    chips = n_row // 2

    to_row = lambda values, distance: lax.ppermute(values, "row", [(i, i ^ distance) for i in range(n_row)])
    to_col = lambda values, distance: lax.ppermute(values, "col", [(i, i ^ distance) for i in range(n_col)])

    col_bits = bits_of(n_col)
    blocks = [[(0, 0), (0, 1)]] + [[(bit, part) for bit in col_bits] for part in range(2) if col_bits]
    far = sorted([d for d in range(n_col) if d & (d - 1)], key=lambda d: (bin(d).count("1"), d))
    blocks += [[(d, 0), (d, 1)] for d in far]

    def bring(panels, members):
        for distance, part in members:
            bit = distance & -distance if part == 0 else 1 << (distance.bit_length() - 1)
            panels[distance, part] = to_col(panels[distance ^ bit, part], bit)

    def piece(ref, owner):
        return ref.at[:, pl.ds(pl.multiple_of(owner * depth, depth), depth)]

    def rows_of(ref, place, extent):
        return ref.at[pl.ds(pl.multiple_of(place * extent, extent), extent)]

    def crossing_moves(sources, results):
        core = lax.axis_index("row") % 2
        return [
            (True, piece(sources[0], 2 * other + 1 - core), rows_of(results[0], other, pieces)) for other in range(chips)
        ]

    def pair_moves(sources, results):
        chip, core = lax.axis_index("row") // 2, lax.axis_index("row") % 2
        moves = []
        for distance in range(chips):
            other = chip ^ distance
            moves.append((True, piece(sources[0], 2 * other + core), rows_of(results[distance], core, pieces)))
            moves.append((True, rows_of(sources[1], other, pieces), rows_of(results[distance], 1 - core, pieces)))
        return moves

    def panel_moves(sources, results):
        chip, moves = lax.axis_index("row") // 2, []
        for distance in range(chips):
            other = chip ^ distance
            for half in range(2):
                target = rows_of(results[half], other % (chips // 2), 2 * pieces)
                moves.append((other // (chips // 2) == half, sources[distance], target))
        return moves

    crossing = place_copies([green_ret], [(chips * pieces, depth)], crossing_moves, "crossing")[0]
    crossing_sent, crossing = crossing, to_row(crossing, 1)
    pairs = place_copies([green_ret, crossing], [(2 * pieces, depth)] * chips, pair_moves, "pairs")
    halves = {(0, part): green_less[:, part * near : (part + 1) * near] for part in range(2)}
    if col_bits:
        halves[0, 0] = hold(halves[0, 0], [crossing_sent])
        bring(halves, blocks[1])
    lesser = {(0, part): (green_less, part) if near % 128 == 0 else (halves[0, part], 0) for part in range(2)}

    order = jnp.asarray(halving_order(n_row), jnp.int32)

    def tiles_of(tile, share, shares):
        count = block // tile // shares
        within = share * count + jnp.arange(count, dtype=jnp.int32)
        return (((order ^ row) * (block // tile))[:, None] + within).reshape(-1)

    after = list(pairs[1:])

    def run(terms, members, tiles, added, tile, name):
        result = sum_of_terms(terms, near * len(members), tiles, added, after, tile, name)
        after[:] = [result]
        return result

    def first_of(members):
        return sigma_ret, [lesser.get(m) or (halves[m], 0) for m in members], False

    def second_of(members):
        return sigma_less, [(mirrored[m], 0) for m in members], True

    def run_first(place):
        return run([first_of(blocks[place])], blocks[place], tiles_of(tile, 0, 1), [], tile, "first_term")

    def run_half(place, kept, share, shares):
        members, height = blocks[place], tile // (2 if place > 1 else 1)
        tiles = tiles_of(height, share, shares)
        half = tiles.shape[0] // 2
        tiles = tiles[half:] if kept else tiles[:half]
        if place in firsts:
            added = [(firsts[place], rows // 2 if kept else 0)]
            return run([second_of(members)], members, tiles, added, height, "second_term")
        return run([first_of(members), second_of(members)], members, tiles, [], height, "both_terms")

    def halve(sums, bits):
        if not bits:
            return sums, bits
        middle = sums[0].shape[0] // 2
        sent = functools.reduce(jnp.add, [array[:middle] for array in sums])
        after.append(sent)
        return [array[middle:] for array in sums] + [to_row(sent, bits[0])], bits[1:]

    row_bits = bits_of(n_row)
    firsts, going = {0: run_first(0)}, []
    if col_bits:
        halves[0, 1] = hold(halves[0, 1], after)
        bring(halves, blocks[2])
        firsts[1] = run_first(1)

    came = [pairs[0]] + [to_row(pairs[distance], 2 * distance) for distance in range(1, chips)]
    shapes = [(columns // 2, depth)] * 2
    panels = place_copies(came, shapes, panel_moves, "mirrored", after)
    mirrored = {(0, part): panels[part] for part in range(2)}
    bring(mirrored, blocks[1] if col_bits else [])

    def relay(panels, part, after):
        for distance in far:
            bit = distance & -distance if part == 0 else 1 << (distance.bit_length() - 1)
            source = distance ^ bit, part
            if source in blocks[1] + blocks[2]:
                panels[source] = hold(panels[source], after)
            bring(panels, [(distance, part)])

    def advance(going, out, places=None):
        last = [which for which, each in enumerate(going) if each is not None and not each[2]]
        last = [which for which in last if places is None or which in places]
        for which, each in enumerate(going):
            if each is not None and each[2] and (places is None or which in places):
                going[which] = [each[0], *halve([hold(each[1][0], after), *each[1][1:]], each[2])]
        for which in last:
            (place, start), sums, _ = going[which]
            going[which] = None
            final = functools.reduce(jnp.add, [hold(sums[0], after), *sums[1:]])
            for index, (distance, part) in enumerate(blocks[place]):
                values = final[:, index * near : (index + 1) * near]
                out = lax.dynamic_update_slice(out, values, (start, (col ^ distance) * columns + part * near))
            after.append(out)
        return out

    def halve_sums(going):
        where, sums, bits = going[0]
        sums = [hold(sums[0], after), *sums[1:]]
        middle = sums[0].shape[0] // 2
        sent = functools.reduce(jnp.add, [array[:middle] for array in sums])
        after.append(sent)
        return sent, [array[middle:] for array in sums]

    def send_later(going, later):
        where, _, bits = going[0]
        sent, kept = later
        going[0] = [where, [*kept, to_row(hold(sent, after), bits[0])], bits[1:]]

    out = jnp.zeros((block, n_col * columns), F32)
    for place, members in enumerate(blocks):
        if place == 1:
            after.extend(halves[member] for member in blocks[2])
            mirrored[0, 1] = hold(mirrored[0, 1], after)
            bring(mirrored, blocks[2])
            relay(halves, 0, after)
        if place == 2:
            after.extend(halves[distance, 0] for distance in far)
            relay(mirrored, 0, after)
            relay(mirrored, 1, after)
            relay(halves, 1, after)
        shares = 2 if place == len(blocks) - 1 and place > 1 else 1
        for share in range(shares):
            sent = run_half(place, False, share, shares)
            came = to_row(sent, 1)
            if place == 2:
                after.extend(halves[distance, 0] for distance in far)
            if share == 1:
                where, sums, bits = going[place - 1]
                going[place - 1] = [where, *halve([hold(sums[0], after), *sums[1:]], bits)]
            kept = run_half(place, True, share, shares)
            now = halve([kept, came], row_bits[1:])
            if place == 1:
                later = halve_sums(going)
            else:
                if place == 2:
                    send_later(going, later)
                    going[1:] = [[each[0], *halve([hold(each[1][0], after), *each[1][1:]], each[2])] for each in going[1:]]
                elif shares == 2 and share == 0:
                    out = advance(going, out, range(place - 1))
                else:
                    out = advance(going, out)
            going.append([(place, share * (block // shares)), *now])
    while any(each is not None for each in going):
        out = advance(going, out)
    return out


def solution(mesh):
    placed = (P("col", "row"), P("col", "row"), P("row", "col"), P(("col", "row"), None))
    return jax.shard_map(
        on_device, mesh=mesh, in_specs=placed, out_specs=P(("col", "row"), None), check_vma=False
    )
```

```python
import functools

import jax
import jax.numpy as jnp
from jax import lax
from jax.experimental import pallas as pl
from jax.experimental.pallas import tpu as pltpu
from jax.sharding import PartitionSpec as P

F32 = jnp.float32
BF16 = jnp.bfloat16


def bits_of(extent):
    assert extent & (extent - 1) == 0
    return [1 << place for place in range(extent.bit_length() - 1)]


def halving_order(extent):
    order = [0]
    for bit in reversed(bits_of(extent)):
        order = [distance | bit for distance in order] + order
    return order


def split(values):
    high = values.astype(BF16)
    return high, (values - high.astype(F32)).astype(BF16)


def term_kernel(kinds, streams, n_parts, n_added, n_after, tiles, *refs):
    held, refs = [], list(refs)

    def take(count):
        taken = refs[:count]
        del refs[:count]
        return taken

    for _ in kinds:
        held.append((take(streams), take(n_parts)))
    added, _, out = take(n_added), take(n_after), take(1)[0]
    panels = [take(2) for _ in kinds]

    @pl.when(pl.program_id(0) == 0)
    def _():
        for mirrored, (_, parts), (high_panel, low_panel) in zip(kinds, held, panels):
            column = 0
            for part in parts:
                columns = slice(column, column + part.shape[0 if mirrored else 1])
                place = (columns, slice(None)) if mirrored else (slice(None), columns)
                high_panel[place], low_panel[place] = split(part[...])
                column = columns.stop

    total = None
    for mirrored, (sigma, _), (high_panel, low_panel) in zip(kinds, held, panels):
        dims = (((1,), (1 if mirrored else 0,)), ((), ()))
        halves = [split(stream[...]) for stream in sigma]
        high, low = [jnp.concatenate([half[which] for half in halves], axis=0) for which in range(2)]
        for left, right in ((high, high_panel), (high, low_panel), (low, high_panel)):
            product = lax.dot_general(left, right[...], dims, preferred_element_type=F32)
            total = product if total is None else total + product
    for other in added:
        total += other[...]
    out[...] = total


def sum_of_terms(terms, columns, tiles, added, after, tile, name):
    depth = terms[0][0].shape[1]
    n_parts = len(terms[0][1])
    near = columns // n_parts
    steps, streams = tiles.shape[0], 1
    in_specs, operands, scratch = [], [], []
    for sigma, parts, mirrored in terms:
        for j in range(streams):
            in_specs.append(pl.BlockSpec((tile // streams, depth), lambda i, t, j=j: (t[i] * streams + j, 0)))
            operands.append(sigma)
        for part, place in parts:
            shape, index = ((near, depth), (place, 0)) if mirrored else ((depth, near), (0, place))
            in_specs.append(pl.BlockSpec(shape, lambda i, t, index=index: index, pipeline_mode=pl.Buffered(1)))
            operands.append(part)
        scratch += [pltpu.VMEM((columns, depth) if mirrored else (depth, columns), BF16)] * 2
    for array, offset in added:
        in_specs.append(pl.BlockSpec((tile, columns), lambda i, t, o=offset // tile: (i + o, 0)))
        operands.append(array)
    in_specs += [pl.BlockSpec(memory_space=pl.ANY) for _ in after]
    kinds = [mirrored for _, _, mirrored in terms]
    return pl.pallas_call(
        functools.partial(term_kernel, kinds, streams, n_parts, len(added), len(after)),
        out_shape=jax.ShapeDtypeStruct((steps * tile, columns), F32),
        grid_spec=pltpu.PrefetchScalarGridSpec(
            num_scalar_prefetch=1,
            grid=(steps,),
            in_specs=in_specs,
            out_specs=pl.BlockSpec((tile, columns), lambda i, t: (i, 0)),
            scratch_shapes=scratch,
        ),
        compiler_params=pltpu.CompilerParams(vmem_limit_bytes=60 << 20),
        cost_estimate=pl.CostEstimate(
            flops=48 * len(terms) * steps * tile * depth * columns,
            bytes_accessed=4 * len(terms) * steps * tile * depth,
            transcendentals=0,
        ),
        name=name,
    )(tiles, *operands, *after)


def place_copies(sources, shapes, moves, name, after=()):
    def kernel(*refs):
        for when, source, target in moves(refs[: len(sources)], refs[len(sources) + len(after) :]):

            @pl.when(when)
            def _(source=source, target=target):
                target[...] = source[...]

    return pl.pallas_call(
        kernel,
        out_shape=[jax.ShapeDtypeStruct(shape, F32) for shape in shapes],
        in_specs=[pl.BlockSpec(memory_space=pltpu.VMEM) for _ in sources]
        + [pl.BlockSpec(memory_space=pl.ANY) for _ in after],
        out_specs=[pl.BlockSpec(memory_space=pltpu.VMEM) for _ in shapes],
        compiler_params=pltpu.CompilerParams(vmem_limit_bytes=60 << 20),
        name=name,
    )(*sources, *after)


def hold(values, after):
    return pl.pallas_call(
        lambda *refs: None,
        out_shape=jax.ShapeDtypeStruct(values.shape, values.dtype),
        in_specs=[pl.BlockSpec(memory_space=pl.ANY)] * (1 + len(after)),
        out_specs=pl.BlockSpec(memory_space=pl.ANY),
        input_output_aliases={0: 0},
        name="hold",
    )(values, *after)


def on_device(sigma_ret, sigma_less, green_less, green_ret):
    n_col, n_row = lax.axis_size("col"), lax.axis_size("row")
    col, row = lax.axis_index("col"), lax.axis_index("row")
    rows, depth = sigma_ret.shape
    columns = green_less.shape[1]
    block, pieces = rows // n_row, green_ret.shape[0]
    tile = min(block, 512)
    near = columns // 2
    chips = n_row // 2

    to_row = lambda values, distance: lax.ppermute(values, "row", [(i, i ^ distance) for i in range(n_row)])
    to_col = lambda values, distance: lax.ppermute(values, "col", [(i, i ^ distance) for i in range(n_col)])

    col_bits = bits_of(n_col)
    blocks = [[(0, 0), (0, 1)]] + [[(bit, part) for bit in col_bits] for part in range(2) if col_bits]
    far = sorted([d for d in range(n_col) if d & (d - 1)], key=lambda d: (bin(d).count("1"), d))
    blocks += [[(d, 0), (d, 1)] for d in far]

    def bring(panels, members):
        for distance, part in members:
            bit = distance & -distance if part == 0 else 1 << (distance.bit_length() - 1)
            panels[distance, part] = to_col(panels[distance ^ bit, part], bit)

    def piece(ref, owner):
        return ref.at[:, pl.ds(pl.multiple_of(owner * depth, depth), depth)]

    def rows_of(ref, place, extent):
        return ref.at[pl.ds(pl.multiple_of(place * extent, extent), extent)]

    def crossing_moves(sources, results):
        core = lax.axis_index("row") % 2
        return [
            (True, piece(sources[0], 2 * other + 1 - core), rows_of(results[0], other, pieces)) for other in range(chips)
        ]

    def pair_moves(sources, results):
        chip, core = lax.axis_index("row") // 2, lax.axis_index("row") % 2
        moves = []
        for distance in range(chips):
            other = chip ^ distance
            moves.append((True, piece(sources[0], 2 * other + core), rows_of(results[distance], core, pieces)))
            moves.append((True, rows_of(sources[1], other, pieces), rows_of(results[distance], 1 - core, pieces)))
        return moves

    def panel_moves(sources, results):
        chip, moves = lax.axis_index("row") // 2, []
        for distance in range(chips):
            other = chip ^ distance
            for half in range(2):
                target = rows_of(results[half], other % (chips // 2), 2 * pieces)
                moves.append((other // (chips // 2) == half, sources[distance], target))
        return moves

    crossing = place_copies([green_ret], [(chips * pieces, depth)], crossing_moves, "crossing")[0]
    crossing_sent, crossing = crossing, to_row(crossing, 1)
    pairs = place_copies([green_ret, crossing], [(2 * pieces, depth)] * chips, pair_moves, "pairs")
    halves = {(0, part): green_less[:, part * near : (part + 1) * near] for part in range(2)}
    if col_bits:
        halves[0, 0] = hold(halves[0, 0], [crossing_sent])
        bring(halves, blocks[1])
    lesser = {(0, part): (green_less, part) if near % 128 == 0 else (halves[0, part], 0) for part in range(2)}

    order = jnp.asarray(halving_order(n_row), jnp.int32)

    def tiles_of(tile, share, shares):
        count = block // tile // shares
        within = share * count + jnp.arange(count, dtype=jnp.int32)
        return (((order ^ row) * (block // tile))[:, None] + within).reshape(-1)

    after = list(pairs[1:])

    def run(terms, members, tiles, added, tile, name):
        result = sum_of_terms(terms, near * len(members), tiles, added, after, tile, name)
        after[:] = [result]
        return result

    def first_of(members):
        return sigma_ret, [lesser.get(m) or (halves[m], 0) for m in members], False

    def second_of(members):
        return sigma_less, [(mirrored[m], 0) for m in members], True

    def run_first(place):
        return run([first_of(blocks[place])], blocks[place], tiles_of(tile, 0, 1), [], tile, "first_term")

    def run_half(place, kept, share, shares):
        members, height = blocks[place], tile // (2 if place > 1 else 1)
        tiles = tiles_of(height, share, shares)
        half = tiles.shape[0] // 2
        tiles = tiles[half:] if kept else tiles[:half]
        if place in firsts:
            added = [(firsts[place], rows // 2 if kept else 0)]
            return run([second_of(members)], members, tiles, added, height, "second_term")
        return run([first_of(members), second_of(members)], members, tiles, [], height, "both_terms")

    def halve(sums, bits):
        if not bits:
            return sums, bits
        middle = sums[0].shape[0] // 2
        sent = functools.reduce(jnp.add, [array[:middle] for array in sums])
        after.append(sent)
        return [array[middle:] for array in sums] + [to_row(sent, bits[0])], bits[1:]

    row_bits = bits_of(n_row)
    firsts, going = {0: run_first(0)}, []
    if col_bits:
        halves[0, 1] = hold(halves[0, 1], after)
        bring(halves, blocks[2])
        firsts[1] = run_first(1)

    came = [pairs[0]] + [to_row(pairs[distance], 2 * distance) for distance in range(1, chips)]
    shapes = [(columns // 2, depth)] * 2
    panels = place_copies(came, shapes, panel_moves, "mirrored", after)
    mirrored = {(0, part): panels[part] for part in range(2)}
    bring(mirrored, blocks[1] if col_bits else [])

    def relay(panels, part, after):
        for distance in far:
            bit = distance & -distance if part == 0 else 1 << (distance.bit_length() - 1)
            source = distance ^ bit, part
            if source in blocks[1] + blocks[2]:
                panels[source] = hold(panels[source], after)
            bring(panels, [(distance, part)])

    def advance(going, out):
        last = [which for which, each in enumerate(going) if each is not None and not each[2]]
        for which, each in enumerate(going):
            if each is not None and each[2]:
                going[which] = [each[0], *halve([hold(each[1][0], after), *each[1][1:]], each[2])]
        for which in last:
            (place, start), sums, _ = going[which]
            going[which] = None
            final = functools.reduce(jnp.add, [hold(sums[0], after), *sums[1:]])
            for index, (distance, part) in enumerate(blocks[place]):
                values = final[:, index * near : (index + 1) * near]
                out = lax.dynamic_update_slice(out, values, (start, (col ^ distance) * columns + part * near))
            after.append(out)
        return out

    def halve_sums(going):
        where, sums, bits = going[0]
        sums = [hold(sums[0], after), *sums[1:]]
        middle = sums[0].shape[0] // 2
        sent = functools.reduce(jnp.add, [array[:middle] for array in sums])
        after.append(sent)
        return sent, [array[middle:] for array in sums]

    def send_later(going, later):
        where, _, bits = going[0]
        sent, kept = later
        going[0] = [where, [*kept, to_row(hold(sent, after), bits[0])], bits[1:]]

    out = jnp.zeros((block, n_col * columns), F32)
    for place, members in enumerate(blocks):
        if place == 1:
            after.extend(halves[member] for member in blocks[2])
            mirrored[0, 1] = hold(mirrored[0, 1], after)
            bring(mirrored, blocks[2])
            relay(halves, 0, after)
        if place == 2:
            relay(mirrored, 0, after)
            relay(mirrored, 1, after)
            relay(halves, 1, after)
        shares = 2 if place == len(blocks) - 1 and place > 1 else 1
        for share in range(shares):
            sent = run_half(place, False, share, shares)
            came = to_row(sent, 1)
            if place == 2:
                after.extend(halves[distance, 0] for distance in far)
            if share == 1:
                out = advance(going, out)
            kept = run_half(place, True, share, shares)
            now = halve([kept, came], row_bits[1:])
            if place == 1:
                later = halve_sums(going)
            else:
                if place == 2:
                    send_later(going, later)
                    going[1:] = [[each[0], *halve([hold(each[1][0], after), *each[1][1:]], each[2])] for each in going[1:]]
                elif shares == 1 or share == 1:
                    out = advance(going, out)
            going.append([(place, share * (block // shares)), *now])
    while any(each is not None for each in going):
        out = advance(going, out)
    return out


def solution(mesh):
    placed = (P("col", "row"), P("col", "row"), P("row", "col"), P(("col", "row"), None))
    return jax.shard_map(
        on_device, mesh=mesh, in_specs=placed, out_specs=P(("col", "row"), None), check_vma=False
    )
```

```python
import functools

import jax
import jax.numpy as jnp
from jax import lax
from jax.experimental import pallas as pl
from jax.experimental.pallas import tpu as pltpu
from jax.sharding import PartitionSpec as P

F32 = jnp.float32
BF16 = jnp.bfloat16


def bits_of(extent):
    assert extent & (extent - 1) == 0
    return [1 << place for place in range(extent.bit_length() - 1)]


def halving_order(extent):
    order = [0]
    for bit in reversed(bits_of(extent)):
        order = [distance | bit for distance in order] + order
    return order


def split(values):
    high = values.astype(BF16)
    return high, (values - high.astype(F32)).astype(BF16)


def term_kernel(kinds, streams, n_parts, n_added, n_after, tiles, *refs):
    held, refs = [], list(refs)

    def take(count):
        taken = refs[:count]
        del refs[:count]
        return taken

    for _ in kinds:
        held.append((take(streams), take(n_parts)))
    added, _, out = take(n_added), take(n_after), take(1)[0]
    panels = [take(2) for _ in kinds]

    @pl.when(pl.program_id(0) == 0)
    def _():
        for mirrored, (_, parts), (high_panel, low_panel) in zip(kinds, held, panels):
            column = 0
            for part in parts:
                columns = slice(column, column + part.shape[0 if mirrored else 1])
                place = (columns, slice(None)) if mirrored else (slice(None), columns)
                high_panel[place], low_panel[place] = split(part[...])
                column = columns.stop

    total = None
    for mirrored, (sigma, _), (high_panel, low_panel) in zip(kinds, held, panels):
        dims = (((1,), (1 if mirrored else 0,)), ((), ()))
        halves = [split(stream[...]) for stream in sigma]
        high, low = [jnp.concatenate([half[which] for half in halves], axis=0) for which in range(2)]
        for left, right in ((high, high_panel), (high, low_panel), (low, high_panel)):
            product = lax.dot_general(left, right[...], dims, preferred_element_type=F32)
            total = product if total is None else total + product
    for other in added:
        total += other[...]
    out[...] = total


def sum_of_terms(terms, columns, tiles, added, after, tile, name):
    depth = terms[0][0].shape[1]
    n_parts = len(terms[0][1])
    near = columns // n_parts
    steps, streams = tiles.shape[0], 1
    in_specs, operands, scratch = [], [], []
    for sigma, parts, mirrored in terms:
        for j in range(streams):
            in_specs.append(pl.BlockSpec((tile // streams, depth), lambda i, t, j=j: (t[i] * streams + j, 0)))
            operands.append(sigma)
        for part, place in parts:
            shape, index = ((near, depth), (place, 0)) if mirrored else ((depth, near), (0, place))
            in_specs.append(pl.BlockSpec(shape, lambda i, t, index=index: index, pipeline_mode=pl.Buffered(1)))
            operands.append(part)
        scratch += [pltpu.VMEM((columns, depth) if mirrored else (depth, columns), BF16)] * 2
    for array, offset in added:
        in_specs.append(pl.BlockSpec((tile, columns), lambda i, t, o=offset // tile: (i + o, 0)))
        operands.append(array)
    in_specs += [pl.BlockSpec(memory_space=pl.ANY) for _ in after]
    kinds = [mirrored for _, _, mirrored in terms]
    return pl.pallas_call(
        functools.partial(term_kernel, kinds, streams, n_parts, len(added), len(after)),
        out_shape=jax.ShapeDtypeStruct((steps * tile, columns), F32),
        grid_spec=pltpu.PrefetchScalarGridSpec(
            num_scalar_prefetch=1,
            grid=(steps,),
            in_specs=in_specs,
            out_specs=pl.BlockSpec((tile, columns), lambda i, t: (i, 0)),
            scratch_shapes=scratch,
        ),
        compiler_params=pltpu.CompilerParams(vmem_limit_bytes=60 << 20),
        cost_estimate=pl.CostEstimate(
            flops=48 * len(terms) * steps * tile * depth * columns,
            bytes_accessed=4 * len(terms) * steps * tile * depth,
            transcendentals=0,
        ),
        name=name,
    )(tiles, *operands, *after)


def place_copies(sources, shapes, moves, name, after=()):
    def kernel(*refs):
        for when, source, target in moves(refs[: len(sources)], refs[len(sources) + len(after) :]):

            @pl.when(when)
            def _(source=source, target=target):
                target[...] = source[...]

    return pl.pallas_call(
        kernel,
        out_shape=[jax.ShapeDtypeStruct(shape, F32) for shape in shapes],
        in_specs=[pl.BlockSpec(memory_space=pltpu.VMEM) for _ in sources]
        + [pl.BlockSpec(memory_space=pl.ANY) for _ in after],
        out_specs=[pl.BlockSpec(memory_space=pltpu.VMEM) for _ in shapes],
        compiler_params=pltpu.CompilerParams(vmem_limit_bytes=60 << 20),
        name=name,
    )(*sources, *after)


def hold(values, after):
    return pl.pallas_call(
        lambda *refs: None,
        out_shape=jax.ShapeDtypeStruct(values.shape, values.dtype),
        in_specs=[pl.BlockSpec(memory_space=pl.ANY)] * (1 + len(after)),
        out_specs=pl.BlockSpec(memory_space=pl.ANY),
        input_output_aliases={0: 0},
        name="hold",
    )(values, *after)


def on_device(sigma_ret, sigma_less, green_less, green_ret):
    n_col, n_row = lax.axis_size("col"), lax.axis_size("row")
    col, row = lax.axis_index("col"), lax.axis_index("row")
    rows, depth = sigma_ret.shape
    columns = green_less.shape[1]
    block, pieces = rows // n_row, green_ret.shape[0]
    tile = min(block, 512)
    near = columns // 2
    chips = n_row // 2

    to_row = lambda values, distance: lax.ppermute(values, "row", [(i, i ^ distance) for i in range(n_row)])
    to_col = lambda values, distance: lax.ppermute(values, "col", [(i, i ^ distance) for i in range(n_col)])

    col_bits = bits_of(n_col)
    blocks = [[(0, 0), (0, 1)]] + [[(bit, part) for bit in col_bits] for part in range(2) if col_bits]
    far = sorted([d for d in range(n_col) if d & (d - 1)], key=lambda d: (bin(d).count("1"), d))
    blocks += [[(d, 0), (d, 1)] for d in far]

    def bring(panels, members):
        for distance, part in members:
            bit = distance & -distance if part == 0 else 1 << (distance.bit_length() - 1)
            panels[distance, part] = to_col(panels[distance ^ bit, part], bit)

    def piece(ref, owner):
        return ref.at[:, pl.ds(pl.multiple_of(owner * depth, depth), depth)]

    def rows_of(ref, place, extent):
        return ref.at[pl.ds(pl.multiple_of(place * extent, extent), extent)]

    def crossing_moves(sources, results):
        core = lax.axis_index("row") % 2
        return [
            (True, piece(sources[0], 2 * other + 1 - core), rows_of(results[0], other, pieces)) for other in range(chips)
        ]

    def pair_moves(sources, results):
        chip, core = lax.axis_index("row") // 2, lax.axis_index("row") % 2
        moves = []
        for distance in range(chips):
            other = chip ^ distance
            moves.append((True, piece(sources[0], 2 * other + core), rows_of(results[distance], core, pieces)))
            moves.append((True, rows_of(sources[1], other, pieces), rows_of(results[distance], 1 - core, pieces)))
        return moves

    def panel_moves(sources, results):
        chip, moves = lax.axis_index("row") // 2, []
        for distance in range(chips):
            other = chip ^ distance
            for half in range(2):
                target = rows_of(results[half], other % (chips // 2), 2 * pieces)
                moves.append((other // (chips // 2) == half, sources[distance], target))
        return moves

    crossing = place_copies([green_ret], [(chips * pieces, depth)], crossing_moves, "crossing")[0]
    crossing_sent, crossing = crossing, to_row(crossing, 1)
    pairs = place_copies([green_ret, crossing], [(2 * pieces, depth)] * chips, pair_moves, "pairs")
    halves = {(0, part): green_less[:, part * near : (part + 1) * near] for part in range(2)}
    if col_bits:
        halves[0, 0] = hold(halves[0, 0], [crossing_sent])
        bring(halves, blocks[1])
    lesser = {(0, part): (green_less, part) if near % 128 == 0 else (halves[0, part], 0) for part in range(2)}

    order = jnp.asarray(halving_order(n_row), jnp.int32)

    def tiles_of(tile, share, shares):
        count = block // tile // shares
        within = share * count + jnp.arange(count, dtype=jnp.int32)
        return (((order ^ row) * (block // tile))[:, None] + within).reshape(-1)

    after = list(pairs[1:])

    def run(terms, members, tiles, added, tile, name):
        result = sum_of_terms(terms, near * len(members), tiles, added, after, tile, name)
        after[:] = [result]
        return result

    def first_of(members):
        return sigma_ret, [lesser.get(m) or (halves[m], 0) for m in members], False

    def second_of(members):
        return sigma_less, [(mirrored[m], 0) for m in members], True

    def run_first(place):
        return run([first_of(blocks[place])], blocks[place], tiles_of(tile, 0, 1), [], tile, "first_term")

    def run_half(place, kept, share, shares):
        members, height = blocks[place], tile // (2 if place > 1 else 1)
        tiles = tiles_of(height, share, shares)
        half = tiles.shape[0] // 2
        tiles = tiles[half:] if kept else tiles[:half]
        if place in firsts:
            added = [(firsts[place], rows // 2 if kept else 0)]
            return run([second_of(members)], members, tiles, added, height, "second_term")
        return run([first_of(members), second_of(members)], members, tiles, [], height, "both_terms")

    def halve(sums, bits):
        if not bits:
            return sums, bits
        middle = sums[0].shape[0] // 2
        sent = functools.reduce(jnp.add, [array[:middle] for array in sums])
        after.append(sent)
        return [array[middle:] for array in sums] + [to_row(sent, bits[0])], bits[1:]

    row_bits = bits_of(n_row)
    firsts, going = {0: run_first(0)}, []
    if col_bits:
        halves[0, 1] = hold(halves[0, 1], after)
        bring(halves, blocks[2])
        firsts[1] = run_first(1)

    came = [pairs[0]] + [to_row(pairs[distance], 2 * distance) for distance in range(1, chips)]
    shapes = [(columns // 2, depth)] * 2
    panels = place_copies(came, shapes, panel_moves, "mirrored", after)
    mirrored = {(0, part): panels[part] for part in range(2)}
    bring(mirrored, blocks[1] if col_bits else [])

    def relay(panels, part, after):
        for distance in far:
            bit = distance & -distance if part == 0 else 1 << (distance.bit_length() - 1)
            source = distance ^ bit, part
            if source in blocks[1] + blocks[2]:
                panels[source] = hold(panels[source], after)
            bring(panels, [(distance, part)])

    def advance(going, out, places=None):
        last = [which for which, each in enumerate(going) if each is not None and not each[2]]
        last = [which for which in last if places is None or which in places]
        for which, each in enumerate(going):
            if each is not None and each[2] and (places is None or which in places):
                going[which] = [each[0], *halve([hold(each[1][0], after), *each[1][1:]], each[2])]
        for which in last:
            (place, start), sums, _ = going[which]
            going[which] = None
            final = functools.reduce(jnp.add, [hold(sums[0], after), *sums[1:]])
            for index, (distance, part) in enumerate(blocks[place]):
                values = final[:, index * near : (index + 1) * near]
                out = lax.dynamic_update_slice(out, values, (start, (col ^ distance) * columns + part * near))
            after.append(out)
        return out

    def halve_sums(going):
        where, sums, bits = going[0]
        sums = [hold(sums[0], after), *sums[1:]]
        middle = sums[0].shape[0] // 2
        sent = functools.reduce(jnp.add, [array[:middle] for array in sums])
        after.append(sent)
        return sent, [array[middle:] for array in sums]

    def send_later(going, later):
        where, _, bits = going[0]
        sent, kept = later
        going[0] = [where, [*kept, to_row(hold(sent, after), bits[0])], bits[1:]]

    out = jnp.zeros((block, n_col * columns), F32)
    for place, members in enumerate(blocks):
        if place == 1:
            after.extend(halves[member] for member in blocks[2])
            mirrored[0, 1] = hold(mirrored[0, 1], after)
            bring(mirrored, blocks[2])
            relay(halves, 0, after)
        if place == 2:
            relay(mirrored, 0, after)
            relay(mirrored, 1, after)
            relay(halves, 1, after)
        shares = 2 if place == len(blocks) - 1 and place > 1 else 1
        for share in range(shares):
            sent = run_half(place, False, share, shares)
            came = to_row(sent, 1)
            if place == 2:
                after.extend(halves[distance, 0] for distance in far)
            if share == 1:
                out = advance(going, out, range(place))
            kept = run_half(place, True, share, shares)
            now = halve([kept, came], row_bits[1:])
            if place == 1:
                later = halve_sums(going)
            else:
                if place == 2:
                    send_later(going, later)
                    going[1:] = [[each[0], *halve([hold(each[1][0], after), *each[1][1:]], each[2])] for each in going[1:]]
                elif shares == 1 or share == 1:
                    out = advance(going, out)
            going.append([(place, share * (block // shares)), *now])
    while any(each is not None for each in going):
        out = advance(going, out)
    return out


def solution(mesh):
    placed = (P("col", "row"), P("col", "row"), P("row", "col"), P(("col", "row"), None))
    return jax.shard_map(
        on_device, mesh=mesh, in_specs=placed, out_specs=P(("col", "row"), None), check_vma=False
    )
```
